512 devices in a mesh: expert: 128 (over y, z, core), hid: 4 (over x).
Axes of the slice: x: 4, y: 8, z: 8, core: 2. Of those that a mesh axis runs over, the one named last changes fastest.
Arguments:
- tokens: bfloat16 [4096, 4096], P('expert'), may hold values from -6 to 6
- routes: int32 [4096, 8], P('expert'), may hold values from 0 to 127, as said below
- member_expert: int32 [32], replicated, may hold values from -1 to 127, as said below
- gate_weight: bfloat16 [131072, 1024], P('expert', 'hid'), may hold values from -0.09375 to 0.09375
- up_weight: bfloat16 [131072, 1024], P('expert', 'hid'), may hold values from -0.09375 to 0.09375
- down_weight: bfloat16 [1024, 131072], P('hid', 'expert'), may hold values from -6 to 6
- ridge: float32 [1024], replicated, may hold values from 20 to 200
Outputs:
- merged: float32 [32768, 1024], P(('expert', 'hid'))
The draws below stay inside these ranges and needn't reach their ends.
Inputs may be any that keep to these rules, and one draw needn't show every extreme that they name: `routes`: each row names 8 distinct experts. Among the rows of one device no expert is named by more than 4 rows, and the expert of one live member slot is named by exactly 4 rows on every device. `member_expert`: -1 marks an empty slot; the live slots of a cluster come first, every cluster has a live slot, some cluster has all 4 live, and live ids are distinct.
All inputs are finite; a program needn't handle non-finite values.
Results may differ from the reference program's by a relative error of at most 0.0057.
Values may be sent and summed in bfloat16 or wider, within the bound.
No kernel may reach another device: no remote copies, remote signals or barrier semaphores. Data moves between devices by JAX's collectives and lax.ppermute only.
A program may use at most 64 MiB of HBM per device.

```python
import math
import jax
import jax.numpy as jnp
from jax import lax

D = 4096
NEXP = 128
TOPK = 8
FF = 1024
DPARTS = 4
TOK_DEV = 32
MPC = 4
CLUSTERS = 8
MEMBERS = 32
CAP = 4
TOKENS = 4096
N_EXPERT = 128


def member_table(key):
    sizes = jax.random.randint(jax.random.fold_in(key, 12), (CLUSTERS,), MPC - 1, MPC + 1)
    busiest = jax.random.randint(jax.random.fold_in(key, 13), (), 0, CLUSTERS)
    sizes = jnp.where(jnp.arange(CLUSTERS) == busiest, MPC, sizes)
    shuffled = jax.random.permutation(jax.random.fold_in(key, 11), NEXP)
    top_place = jnp.argmax((shuffled == NEXP - 1).astype(jnp.int32)).astype(jnp.int32)
    slot_place = (busiest * MPC + 1).astype(jnp.int32)
    displaced = shuffled[slot_place]
    shuffled = shuffled.at[top_place].set(displaced)
    shuffled = shuffled.at[slot_place].set(NEXP - 1)
    shuffled = shuffled[:MEMBERS]
    slot_index = jnp.arange(MEMBERS) % MPC
    live = slot_index < sizes[jnp.arange(MEMBERS) // MPC]
    table = jnp.where(live, shuffled, -1).astype(jnp.int32)
    return (table, shuffled[busiest * MPC])


def route_block(subkey, target):
    unit = TOK_DEV // 16
    leading = NEXP // 4
    middle = NEXP // 2
    order = jax.random.permutation(jax.random.fold_in(subkey, 1), NEXP)
    order = jnp.where(order == target, order[0], order)
    order = order.at[0].set(target)
    extra = jax.random.randint(jax.random.fold_in(subkey, 2), (), 0, leading + 1)
    ranks = jnp.arange(NEXP)
    counts = jnp.where(ranks < leading + extra, 2 * unit, jnp.where(ranks < leading + middle - extra, unit, 0))
    ends = jnp.cumsum(counts)
    labels = jnp.arange(TOK_DEV * TOPK)
    rank_of = jnp.searchsorted(ends, labels, side='right')
    experts = order[rank_of].reshape(TOPK, TOK_DEV).T
    shuffle = jax.random.permutation(jax.random.fold_in(subkey, 3), TOK_DEV)
    return experts[shuffle]


def draw_routes(key, part):
    table, target = member_table(key)
    key = jax.random.fold_in(key, 5)
    subkeys = jax.random.split(key, TOKENS // TOK_DEV)
    routed = jax.vmap(route_block, in_axes=(0, None))(subkeys, target)
    return routed.reshape(TOKENS, TOPK).astype(jnp.int32)


def draw_member_expert(key, part):
    table, target = member_table(key)
    return table


def block_levels(stream_key, shape, shards, least, largest):
    factor_of, own = 1.0, jax.random.fold_in(stream_key, 6)
    for dim, shards_of in shards:
        draws = jnp.exp(jax.random.uniform(jax.random.fold_in(own, dim), (shards_of,), jnp.float32, least / len(shards), largest / len(shards)))
        factor_of = factor_of * jnp.repeat(draws, shape[dim] // shards_of).reshape([-1 if axis == dim else 1 for axis in range(len(shape))])
    return factor_of


def gaussian(own_key, dims, deviation, bound, cuts=(), kind=jnp.bfloat16):
    array = jax.random.normal(own_key, dims, jnp.float32) * deviation
    if len(cuts) > 0:
        array = block_levels(own_key, dims, cuts, -0.22, 0.18) * array
    return jnp.clip(array, min=-bound, max=bound).astype(kind)


def setup_inputs(seed: int = 0) -> dict:
    key_list = jax.random.split(jax.random.key(seed), 8)
    return {
        "tokens": gaussian(key_list[0], (TOKENS, D), 1.0, 6.0, ((0, 128),)),
        "routes": draw_routes(jax.random.fold_in(key_list[7], 71), 0),
        "member_expert": draw_member_expert(jax.random.fold_in(key_list[7], 71), 0),
        "gate_weight": gaussian(key_list[3], (MEMBERS * D, FF), D ** -0.5, 0.09375, ((0, 128), (1, 4))),
        "up_weight": gaussian(key_list[4], (MEMBERS * D, FF), D ** -0.5, 0.09375, ((0, 128), (1, 4))),
        "down_weight": gaussian(key_list[5], (FF, MEMBERS * D), 1.0, 6.0, ((0, 4), (1, 128))),
        "ridge": jnp.clip(jnp.exp(jax.random.uniform(key_list[6], (FF,), jnp.float32, math.log(20.0), math.log(200.0))), 20.0, 200.0),
    }


def reference(tokens, routes, member_expert, gate_weight, up_weight, down_weight, ridge):
    quarter = D // DPARTS
    slots = N_EXPERT * CAP
    gate_split = gate_weight.reshape(CLUSTERS, DPARTS, MPC, quarter, FF)
    up_split = up_weight.reshape(CLUSTERS, DPARTS, MPC, quarter, FF)
    down_split = jnp.transpose(down_weight.reshape(FF, CLUSTERS, DPARTS, MPC, quarter), (1, 0, 2, 3, 4))
    token_index = jnp.arange(TOKENS, dtype=jnp.int32)

    def member_terms(expert_id, gate_proj, up_proj, down_proj):
        chosen = jnp.any(routes == expert_id, axis=1).astype(jnp.int32)
        position = jnp.cumsum(chosen) - 1
        position = jnp.where(chosen > 0, position, slots).astype(jnp.int32)
        source_row = jnp.zeros((slots,), jnp.int32).at[position].set(token_index, mode='drop')
        filled = jnp.zeros((slots,), jnp.int32).at[position].set(1, mode='drop')
        member_rows = jnp.where(filled[:, None] > 0, tokens[source_row], jnp.zeros((), tokens.dtype))
        gate_value = jnp.dot(member_rows.astype(jnp.float32), gate_proj.astype(jnp.float32), preferred_element_type=jnp.float32)
        up_value = jnp.dot(member_rows.astype(jnp.float32), up_proj.astype(jnp.float32), preferred_element_type=jnp.float32)
        hidden = (jax.nn.silu(gate_value) * up_value).astype(jnp.bfloat16)
        gram = jnp.dot(hidden.T.astype(jnp.float32), hidden.astype(jnp.float32), preferred_element_type=jnp.float32)
        outputs = jnp.dot(hidden.astype(jnp.float32), down_proj.astype(jnp.float32), preferred_element_type=jnp.float32).astype(jnp.bfloat16)
        cross = jnp.dot(hidden.T.astype(jnp.float32), outputs.astype(jnp.float32), preferred_element_type=jnp.float32)
        return (gram, cross)

    def cluster_solve(inputs):
        experts, gate_block, up_block, down_block = inputs
        gram_total = jnp.zeros((FF, FF), jnp.float32)
        cross_total = jnp.zeros((FF, D), jnp.float32)
        for slot_index in range(MPC):
            gram, cross = member_terms(experts[slot_index], gate_block[:, slot_index].reshape(D, FF), up_block[:, slot_index].reshape(D, FF), down_block[:, :, slot_index].reshape(FF, D))
            gram_total = gram_total + gram
            cross_total = cross_total + cross
        system = gram_total + jnp.diag(ridge)
        factor = jnp.linalg.cholesky(system)
        solved = jax.scipy.linalg.cho_solve((factor, True), cross_total)
        return solved.T
    result = lax.map(cluster_solve, (member_expert.reshape(CLUSTERS, MPC), gate_split, up_split, down_split))
    return result.reshape(CLUSTERS * D, FF)
```

```python
import functools

import jax
import jax.numpy as jnp
from jax import lax
from jax.experimental import pallas as pl
from jax.experimental.pallas import tpu as pltpu
from jax.sharding import Mesh
from jax.sharding import PartitionSpec as P

f32 = jnp.float32
bf16 = jnp.bfloat16
EXPERT = ("y", "p", "z0", "core")
BLOCK = 128


def sub_bc(v,k): return jnp.broadcast_to(v[k:k+1,:],v.shape)
def lane_bc(v,m): return jnp.broadcast_to(v[:,m:m+1],v.shape)
def tree_sum(t):
    while len(t)>1: t=[t[i]+t[i+1] for i in range(0,len(t)-1,2)]+([t[-1]] if len(t)%2 else [])
    return t[0]
def mm(a,b,dims=((1,),(0,)),precision=lax.Precision.HIGHEST):
    return lax.dot_general(a,b,(dims,((),())),preferred_element_type=f32,precision=precision)

def panel_step(rows,own,others,j0,sub,lane):
    q=len(own); w=8*q
    cols=[[lane_bc(rows[v],j0+m) for v in own] for m in range(w)]
    mult={v:[lane_bc(rows[v],j0+m) for m in range(w)] for v in others}
    panel=(lane>=j0)&(lane<j0+w)
    top=[jnp.where(panel,(lane-j0-8*a==sub).astype(f32),rows[v]) for a,v in enumerate(own)]
    for k in range(w):
        ka,ks=divmod(k,8)
        here=sub==ks
        r=1.0/sub_bc(cols[k][ka],ks)
        piv=[(jnp.where(here,-1.0,c) if a==ka else c) for a,c in enumerate(cols[k])]
        pr=[c*r for c in piv]
        def step(vs,late=False):
            t=sub_bc(vs[ka],ks)
            x0=[jnp.where(here,0.0,x) if a==ka else x for a,x in enumerate(vs)]
            if late: return [x-(piv[a]*t)*r for a,x in enumerate(x0)]
            return [x-pr[a]*t for a,x in enumerate(x0)]
        for m in range(k+1,w): cols[m]=step(cols[m],m==k+1)
        top=step(top)
    for a,v in enumerate(own): rows[v]=top[a]
    if others:
        spread=[sub_bc(top[m//8],m%8) for m in range(w)]
        for v in others:
            rows[v]=jnp.where(panel,0.0,rows[v])-tree_sum([mult[v][m]*spread[m] for m in range(w)])

def invert_block(rows,q,s):
    n=len(rows); rows=list(rows)
    sub=lax.broadcasted_iota(jnp.int32,(8,BLOCK),0); lane=lax.broadcasted_iota(jnp.int32,(8,BLOCK),1)
    for a in range(0,n,s):
        strip=list(range(a,a+s))
        for t in range(a,a+s,q):
            own=list(range(t,t+q))
            panel_step(rows,own,[v for v in strip if v not in own],8*t,sub,lane)
        rest=[v for v in range(n) if v not in strip]
        if rest:
            z=jnp.zeros((8,BLOCK),f32)
            wide=jnp.concatenate([rows[v] if v in strip else z for v in range(n)],0)
            lhs=jnp.concatenate([rows[v] for v in rest],0)
            upd=mm(lhs,wide)
            inst=(lane>=8*a)&(lane<8*(a+s))
            for i,v in enumerate(rest):
                rows[v]=jnp.where(inst,0.0,rows[v])-upd[8*i:8*i+8]
    return rows

def fused_kernel(q,s,h_ref,d_ref,ridge_ref,o_ref,a_ref,u_ref,w_ref,y_ref):
    n=h_ref.shape[1]; nb=n//BLOCK; nc=d_ref.shape[2]; slots=d_ref.shape[0]
    parts=h_ref.shape[0]//(slots*BLOCK)
    sub=lax.broadcasted_iota(jnp.int32,(8,BLOCK),0); lane=lax.broadcasted_iota(jnp.int32,(8,BLOCK),1)
    def gram(k):
        lhs=h_ref[:,k*BLOCK:(k+1)*BLOCK].T
        a_ref[k*BLOCK:(k+1)*BLOCK,k*BLOCK:n]=mm(lhs,h_ref[:,k*BLOCK:],precision=None)
        return lhs
    def cross(k,lhs): a_ref[k*BLOCK:(k+1)*BLOCK,n:n+nc]=mm(lhs,y_ref[...],precision=None)
    l0=gram(0)
    for i in range(slots):
        rows=jnp.concatenate([h_ref[(p*slots+i)*BLOCK:(p*slots+i+1)*BLOCK,:] for p in range(parts)],0)
        y=mm(rows,d_ref[i],precision=None).astype(bf16)
        for p in range(parts): y_ref[(p*slots+i)*BLOCK:(p*slots+i+1)*BLOCK,:]=y[p*BLOCK:(p+1)*BLOCK]
    cross(0,l0)
    for k in range(nb):
        r0,r1,r2=k*BLOCK,(k+1)*BLOCK,(k+2)*BLOCK
        if k+1<nb:
            lhs=gram(k+1); cross(k+1,lhs)
            if k>0:
                a_ref[r1:r2,r1:n+nc]-=mm(u_ref[:r0,r1:r2],w_ref[:r0,r1:n+nc],((0,),(0,)))
        tiles=[]
        for v in range(BLOCK//8):
            t=a_ref[r0+8*v:r0+8*v+8,r0:r1]
            tiles.append(jnp.where(lane-8*v==sub,t+ridge_ref[0:1,r0:r1],t))
        inv=jnp.concatenate(invert_block(tiles,q,s),0)
        u=a_ref[r0:r1,r1:n+nc]
        w=mm(inv,u)
        u_ref[r0:r1,r1:n+nc]=u
        w_ref[r0:r1,r1:n+nc]=w
        if k+1<nb:
            a_ref[r1:r2,r1:n+nc]-=mm(u[:,:BLOCK],w,((0,),(0,)))
    xs={}
    for k in range(nb-1,-1,-1):
        r0,r1,r2=k*BLOCK,(k+1)*BLOCK,(k+2)*BLOCK
        x=w_ref[r0:r1,n:n+nc]
        if k+2<nb: x=x-mm(w_ref[r0:r1,r2:n],jnp.concatenate([xs[j] for j in range(k+2,nb)],0))
        if k+1<nb: x=x-mm(w_ref[r0:r1,r1:r2],xs[k+1])
        xs[k]=x
        o_ref[:,r0:r1]=x.T

def fused_solve(h,d,ridge,q=2,s=4):
    n=h.shape[1]; nc=d.shape[2]
    return pl.pallas_call(functools.partial(fused_kernel,q,s),out_shape=jax.ShapeDtypeStruct((nc,n),f32),
        in_specs=[pl.BlockSpec(memory_space=pltpu.VMEM)]*3,out_specs=pl.BlockSpec(memory_space=pltpu.VMEM),
        scratch_shapes=[pltpu.VMEM((n,n+BLOCK),f32)]*3+[pltpu.VMEM((h.shape[0],nc),bf16)],
        compiler_params=pltpu.CompilerParams(vmem_limit_bytes=44*2**20))(h,d,ridge.reshape(1,n))


def shifted(a, axis, distance):
    n = lax.axis_size(axis)
    return lax.ppermute(a, axis, [(i, (i + distance) % n) for i in range(n)])


def gather_x(a):
    n = a.shape[0]
    x = lax.axis_index("x")
    up, down = shifted(a, "x", 1), shifted(a, "x", -1)
    far_a = shifted(up[: n // 2], "x", 1)
    far_b = shifted(down[n // 2 :], "x", -1)
    out = jnp.zeros((4 * n, a.shape[1]), a.dtype)
    far = jnp.concatenate([far_a, far_b], 0)
    for d, block in ((0, a), (3, up), (1, down), (2, far)):
        out = lax.dynamic_update_slice(out, block, ((x + d) % 4 * n, 0))
    return out


def per_device(tokens, routes, member_expert, gate_weight, up_weight, down_weight, ridge):
    x = lax.axis_index("x")
    count, width = tokens.shape
    hidden = gate_weight.shape[1]
    chosen = jnp.any(routes[:, :, None] == member_expert[None, None, :], axis=1)
    chosen = chosen.astype(f32)
    triangle = jnp.tril(jnp.ones((count, count), f32))
    position = jnp.dot(triangle, chosen, preferred_element_type=f32) - 1.0
    selector = chosen * (position == x.astype(f32)).astype(f32)
    rows = jnp.dot(selector.T.astype(bf16), tokens, preferred_element_type=f32).astype(bf16)
    outgoing = rows.reshape(8, 4, 4, width // 4).transpose(0, 2, 1, 3).reshape(128, width // 4)
    received = lax.all_to_all(outgoing, EXPERT, 0, 0, tiled=True)
    slot_rows = gather_x(received)
    gate = jnp.dot(slot_rows, gate_weight, preferred_element_type=f32)
    up = jnp.dot(slot_rows, up_weight, preferred_element_type=f32)
    partial = jnp.concatenate([gate, up], 1)
    span = partial.shape[0] // 4
    parts = lax.all_to_all(partial, "p", 0, 0, tiled=True)
    total = jnp.sum(parts.reshape(4, span, 2 * hidden), axis=0)
    h_own = (jax.nn.silu(total[:, :hidden]) * total[:, hidden:]).astype(bf16)
    h_rows = lax.all_gather(h_own, "x", axis=1, tiled=True)
    down, h_rows = lax.optimization_barrier((down_weight, h_rows))
    h = lax.all_gather(h_rows, ("p", "z0", "core"), axis=0, tiled=True)
    down = down.reshape(down.shape[0], 16, 64).transpose(1, 0, 2)
    down = lax.all_to_all(down, ("z0", "core", "x"), 0, 0, tiled=True)
    down = down.reshape(4, 4 * hidden, 64)
    return fused_solve(h, down, ridge)


def solution(mesh):
    fine = Mesh(mesh.devices.reshape(8, 4, 2, 2, 4), ("y", "p", "z0", "core", "x"))
    in_specs = (
        P(EXPERT, None),
        P(EXPERT, None),
        P(),
        P(EXPERT, "x"),
        P(EXPERT, "x"),
        P("x", EXPERT),
        P(),
    )
    return jax.shard_map(
        per_device,
        mesh=fine,
        in_specs=in_specs,
        out_specs=P(EXPERT + ("x",), None),
        check_vma=False,
    )
```

```python
import functools

import jax
import jax.numpy as jnp
from jax import lax
from jax.experimental import pallas as pl
from jax.experimental.pallas import tpu as pltpu
from jax.sharding import Mesh
from jax.sharding import PartitionSpec as P

f32 = jnp.float32
bf16 = jnp.bfloat16
EXPERT = ("y", "p", "z0", "core")
BLOCK = 128


def sub_bc(v,k): return jnp.broadcast_to(v[k:k+1,:],v.shape)
def lane_bc(v,m): return jnp.broadcast_to(v[:,m:m+1],v.shape)
def tree_sum(t):
    while len(t)>1: t=[t[i]+t[i+1] for i in range(0,len(t)-1,2)]+([t[-1]] if len(t)%2 else [])
    return t[0]
def mm(a,b,dims=((1,),(0,)),precision=lax.Precision.HIGHEST):
    return lax.dot_general(a,b,(dims,((),())),preferred_element_type=f32,precision=precision)

def panel_step(rows,own,others,j0,sub,lane):
    q=len(own); w=8*q
    cols=[[lane_bc(rows[v],j0+m) for v in own] for m in range(w)]
    mult={v:[lane_bc(rows[v],j0+m) for m in range(w)] for v in others}
    panel=(lane>=j0)&(lane<j0+w)
    top=[jnp.where(panel,(lane-j0-8*a==sub).astype(f32),rows[v]) for a,v in enumerate(own)]
    for k in range(w):
        ka,ks=divmod(k,8)
        here=sub==ks
        r=1.0/sub_bc(cols[k][ka],ks)
        piv=[(jnp.where(here,-1.0,c) if a==ka else c) for a,c in enumerate(cols[k])]
        pr=[c*r for c in piv]
        def step(vs,late=False):
            t=sub_bc(vs[ka],ks)
            x0=[jnp.where(here,0.0,x) if a==ka else x for a,x in enumerate(vs)]
            if late: return [x-(piv[a]*t)*r for a,x in enumerate(x0)]
            return [x-pr[a]*t for a,x in enumerate(x0)]
        for m in range(k+1,w): cols[m]=step(cols[m],m==k+1)
        top=step(top)
    for a,v in enumerate(own): rows[v]=top[a]
    if others:
        spread=[sub_bc(top[m//8],m%8) for m in range(w)]
        for v in others:
            rows[v]=jnp.where(panel,0.0,rows[v])-tree_sum([mult[v][m]*spread[m] for m in range(w)])

def invert_block(rows,q,s):
    n=len(rows); rows=list(rows)
    sub=lax.broadcasted_iota(jnp.int32,(8,BLOCK),0); lane=lax.broadcasted_iota(jnp.int32,(8,BLOCK),1)
    for a in range(0,n,s):
        strip=list(range(a,a+s))
        for t in range(a,a+s,q):
            own=list(range(t,t+q))
            panel_step(rows,own,[v for v in strip if v not in own],8*t,sub,lane)
        rest=[v for v in range(n) if v not in strip]
        if rest:
            z=jnp.zeros((8,BLOCK),f32)
            wide=jnp.concatenate([rows[v] if v in strip else z for v in range(n)],0)
            lhs=jnp.concatenate([rows[v] for v in rest],0)
            upd=mm(lhs,wide)
            inst=(lane>=8*a)&(lane<8*(a+s))
            for i,v in enumerate(rest):
                rows[v]=jnp.where(inst,0.0,rows[v])-upd[8*i:8*i+8]
    return rows

def fused_kernel(q,s,place_ref,own_ref,down_ref,up_ref,far_a_ref,far_b_ref,own_e_ref,near_e_ref,far_e_ref,d_ref,ridge_ref,o_ref,h_ref,a_ref,u_ref,w_ref,y_ref):
    x,core=place_ref[0],place_ref[1]
    half,wide=own_ref.shape
    part=half//2
    def cols(d): return pl.ds(pl.multiple_of((x+d)%4*wide,wide),wide)
    h_ref[:half,cols(0)]=own_ref[...]
    h_ref[half:,cols(0)]=own_e_ref[...]
    h_ref[:half,cols(3)]=down_ref[...]
    h_ref[half:,cols(3)]=near_e_ref[:half]
    h_ref[:half,cols(1)]=up_ref[...]
    h_ref[half:,cols(1)]=near_e_ref[half:]
    h_ref[:part,cols(2)]=far_a_ref[...]
    h_ref[part:half,cols(2)]=far_b_ref[...]
    h_ref[half:,cols(2)]=far_e_ref[...]
    n=h_ref.shape[1]; nb=n//BLOCK; nc=d_ref.shape[2]; slots=d_ref.shape[0]
    parts=h_ref.shape[0]//(slots*BLOCK)
    sub=lax.broadcasted_iota(jnp.int32,(8,BLOCK),0); lane=lax.broadcasted_iota(jnp.int32,(8,BLOCK),1)
    def gram(k):
        lhs=h_ref[:,k*BLOCK:(k+1)*BLOCK].T
        a_ref[k*BLOCK:(k+1)*BLOCK,k*BLOCK:n]=mm(lhs,h_ref[:,k*BLOCK:],precision=None)
        return lhs
    def cross(k,lhs): a_ref[k*BLOCK:(k+1)*BLOCK,n:n+nc]=mm(lhs,y_ref[...],precision=None)
    l0=gram(0)
    for side in range(2):
        for z0 in range(2):
            starts=[side*half+(p*2+z0)*BLOCK for p in range(parts)]
            rows=jnp.concatenate([h_ref[r:r+BLOCK,:] for r in starts],0)
            slot=2*z0+(core if side==0 else 1-core)
            y=mm(rows,d_ref[slot],precision=None).astype(bf16)
            for p,r in enumerate(starts): y_ref[r:r+BLOCK,:]=y[p*BLOCK:(p+1)*BLOCK]
    cross(0,l0)
    for k in range(nb):
        r0,r1,r2=k*BLOCK,(k+1)*BLOCK,(k+2)*BLOCK
        if k+1<nb:
            lhs=gram(k+1); cross(k+1,lhs)
            if k>0:
                a_ref[r1:r2,r1:n+nc]-=mm(u_ref[:r0,r1:r2],w_ref[:r0,r1:n+nc],((0,),(0,)))
        tiles=[]
        for v in range(BLOCK//8):
            t=a_ref[r0+8*v:r0+8*v+8,r0:r1]
            tiles.append(jnp.where(lane-8*v==sub,t+ridge_ref[0:1,r0:r1],t))
        inv=jnp.concatenate(invert_block(tiles,q,s),0)
        u=a_ref[r0:r1,r1:n+nc]
        w=mm(inv,u)
        u_ref[r0:r1,r1:n+nc]=u
        w_ref[r0:r1,r1:n+nc]=w
        if k+1<nb:
            a_ref[r1:r2,r1:n+nc]-=mm(u[:,:BLOCK],w,((0,),(0,)))
    xs={}
    for k in range(nb-1,-1,-1):
        r0,r1,r2=k*BLOCK,(k+1)*BLOCK,(k+2)*BLOCK
        x=w_ref[r0:r1,n:n+nc]
        if k+2<nb: x=x-mm(w_ref[r0:r1,r2:n],jnp.concatenate([xs[j] for j in range(k+2,nb)],0))
        if k+1<nb: x=x-mm(w_ref[r0:r1,r1:r2],xs[k+1])
        xs[k]=x
        o_ref[:,r0:r1]=x.T

def fused_solve(place,blocks,d,ridge,q=2,s=4):
    n=d.shape[1]; nc=d.shape[2]
    vmem=pl.BlockSpec(memory_space=pltpu.VMEM)
    return pl.pallas_call(functools.partial(fused_kernel,q,s),out_shape=jax.ShapeDtypeStruct((nc,n),f32),
        in_specs=[pl.BlockSpec(memory_space=pltpu.SMEM)]+[vmem]*10,out_specs=vmem,
        scratch_shapes=[pltpu.VMEM((2*blocks[0].shape[0],n),bf16)]+[pltpu.VMEM((n,n+BLOCK),f32)]*3+[pltpu.VMEM((2*blocks[0].shape[0],nc),bf16)],
        compiler_params=pltpu.CompilerParams(vmem_limit_bytes=46*2**20))(place,*blocks,d,ridge.reshape(1,n))


def shifted(a, axis, distance):
    n = lax.axis_size(axis)
    return lax.ppermute(a, axis, [(i, (i + distance) % n) for i in range(n)])


def per_device(tokens, routes, member_expert, gate_weight, up_weight, down_weight, ridge):
    count, width = tokens.shape
    hidden = gate_weight.shape[1]
    cap, quarter = 4, width // 4
    down = down_weight.reshape(hidden, 16, 64).transpose(1, 0, 2)
    down = lax.all_to_all(down, ("z0", "core", "x"), 0, 0, tiled=True)
    down = down.reshape(4, 4 * hidden, 64)
    chosen = jnp.any(routes[:, :, None] == member_expert[None, None, :], axis=1).astype(f32)
    triangle = jnp.tril(jnp.ones((count, count), f32))
    position = jnp.dot(triangle, chosen, preferred_element_type=f32) - 1.0
    selector = chosen.T[:, None, :] * (
        position.T[:, None, :] == jnp.arange(cap, dtype=f32)[None, :, None]
    )
    outgoing = jnp.einsum(
        "cist,tqd->cqisd",
        selector.astype(bf16).reshape(8, 4, cap, count),
        tokens.reshape(count, 4, quarter),
        preferred_element_type=f32,
    )
    outgoing = outgoing.astype(bf16).reshape(128, cap, quarter)
    received = lax.all_to_all(outgoing, EXPERT, 0, 0, tiled=True)
    slot_rows = received.reshape(128 * cap, quarter)
    gate = jnp.dot(slot_rows, gate_weight, preferred_element_type=f32)
    up = jnp.dot(slot_rows, up_weight, preferred_element_type=f32)
    partial = jnp.concatenate([gate, up], 1)
    span = partial.shape[0] // 4
    parts = lax.all_to_all(partial, "p", 0, 0, tiled=True)
    total = jnp.sum(parts.reshape(4, span, 2 * hidden), axis=0)
    h_own = (jax.nn.silu(total[:, :hidden]) * total[:, hidden:]).astype(bf16)
    copies = jnp.broadcast_to(h_own[None], (8, span, hidden)).reshape(8 * span, hidden)
    own = lax.all_to_all(copies, ("p", "z0"), 0, 0, tiled=True)
    from_below, from_above = shifted(own, "x", 1), shifted(own, "x", -1)
    own_e = shifted(own, "core", 1)
    far_a = shifted(from_below[: 4 * span], "x", 1)
    far_b = shifted(from_above[4 * span :], "x", -1)
    near_e = shifted(jnp.concatenate([from_below, from_above], 0), "core", 1)
    far_e = shifted(jnp.concatenate([far_a, far_b], 0), "core", 1)
    place = jnp.stack([lax.axis_index("x"), lax.axis_index("core")]).astype(jnp.int32)
    blocks = [own, from_below, from_above, far_a, far_b, own_e, near_e, far_e]
    return fused_solve(place, blocks, down, ridge)


def solution(mesh):
    fine = Mesh(mesh.devices.reshape(8, 4, 2, 2, 4), ("y", "p", "z0", "core", "x"))
    in_specs = (
        P(EXPERT, None),
        P(EXPERT, None),
        P(),
        P(EXPERT, "x"),
        P(EXPERT, "x"),
        P("x", EXPERT),
        P(),
    )
    return jax.shard_map(
        per_device,
        mesh=fine,
        in_specs=in_specs,
        out_specs=P(EXPERT + ("x",), None),
        check_vma=False,
    )
```

```python
import functools

import jax
import jax.numpy as jnp
from jax import lax
from jax.experimental import pallas as pl
from jax.experimental.pallas import tpu as pltpu
from jax.sharding import Mesh
from jax.sharding import PartitionSpec as P

f32 = jnp.float32
bf16 = jnp.bfloat16
EXPERT = ("y", "p", "z0", "core")
BLOCK = 128


def sub_bc(v,k): return jnp.broadcast_to(v[k:k+1,:],v.shape)
def lane_bc(v,m): return jnp.broadcast_to(v[:,m:m+1],v.shape)
def tree_sum(t):
    while len(t)>1: t=[t[i]+t[i+1] for i in range(0,len(t)-1,2)]+([t[-1]] if len(t)%2 else [])
    return t[0]
def mm(a,b,dims=((1,),(0,)),precision=lax.Precision.HIGHEST):
    return lax.dot_general(a,b,(dims,((),())),preferred_element_type=f32,precision=precision)

def panel_step(rows,own,others,j0,sub,lane):
    q=len(own); w=8*q
    cols=[[lane_bc(rows[v],j0+m) for v in own] for m in range(w)]
    mult={v:[lane_bc(rows[v],j0+m) for m in range(w)] for v in others}
    panel=(lane>=j0)&(lane<j0+w)
    top=[jnp.where(panel,(lane-j0-8*a==sub).astype(f32),rows[v]) for a,v in enumerate(own)]
    for k in range(w):
        ka,ks=divmod(k,8)
        here=sub==ks
        r=1.0/sub_bc(cols[k][ka],ks)
        piv=[(jnp.where(here,-1.0,c) if a==ka else c) for a,c in enumerate(cols[k])]
        pr=[c*r for c in piv]
        def step(vs,late=False):
            t=sub_bc(vs[ka],ks)
            x0=[jnp.where(here,0.0,x) if a==ka else x for a,x in enumerate(vs)]
            if late: return [x-(piv[a]*t)*r for a,x in enumerate(x0)]
            return [x-pr[a]*t for a,x in enumerate(x0)]
        for m in range(k+1,w): cols[m]=step(cols[m],m==k+1)
        top=step(top)
    for a,v in enumerate(own): rows[v]=top[a]
    if others:
        spread=[sub_bc(top[m//8],m%8) for m in range(w)]
        for v in others:
            rows[v]=jnp.where(panel,0.0,rows[v])-tree_sum([mult[v][m]*spread[m] for m in range(w)])

def invert_block(rows,q,s):
    n=len(rows); rows=list(rows)
    sub=lax.broadcasted_iota(jnp.int32,(8,BLOCK),0); lane=lax.broadcasted_iota(jnp.int32,(8,BLOCK),1)
    for a in range(0,n,s):
        strip=list(range(a,a+s))
        for t in range(a,a+s,q):
            own=list(range(t,t+q))
            panel_step(rows,own,[v for v in strip if v not in own],8*t,sub,lane)
        rest=[v for v in range(n) if v not in strip]
        if rest:
            z=jnp.zeros((8,BLOCK),f32)
            wide=jnp.concatenate([rows[v] if v in strip else z for v in range(n)],0)
            lhs=jnp.concatenate([rows[v] for v in rest],0)
            upd=mm(lhs,wide)
            inst=(lane>=8*a)&(lane<8*(a+s))
            for i,v in enumerate(rest):
                rows[v]=jnp.where(inst,0.0,rows[v])-upd[8*i:8*i+8]
    return rows


class Parts:
    def __init__(self): self.groups=[]
    def add(self,first,count,u,w,inv): self.groups.append((first,count,u,w,inv))
    def find(self,k): return next(g for g in self.groups if g[0]<=k<g[0]+g[1])
    def column(self,k,rows):
        g=self.find(k); c=(k-g[0])*BLOCK
        return g[2][:rows*BLOCK,c:c+BLOCK]
    def inverse(self,k):
        g=self.find(k); r=(k-g[0])*BLOCK
        return g[4][r:r+BLOCK,:]

def gather(pieces,c0,c1): return jnp.concatenate([p[:,c0:c1] for p in pieces],0)

def grow(parts,first,count,pieces_of,ridge,u,w,inv,a,g,q,s,rhs=None):
    sub=lax.broadcasted_iota(jnp.int32,(8,BLOCK),0); lane=lax.broadcasted_iota(jnp.int32,(8,BLOCK),1)
    wide=count*BLOCK; all_cols=wide+(rhs[0].shape[0] if rhs is not None else 0)
    turned=jnp.concatenate([gather(pieces_of(first+2*j),0,2*BLOCK) for j in range(count//2)],1).T
    for b in range((first+count)//2):
        g[:,2*b*BLOCK:2*(b+1)*BLOCK]=mm(turned,gather(pieces_of(2*b),0,2*BLOCK),precision=None)
        if rhs is not None: rhs[1][:,2*b*BLOCK:2*(b+1)*BLOCK]=mm(rhs[0][...],gather(pieces_of(2*b),0,2*BLOCK),precision=None)
    def product(k,c0):
        out=[g[:,k*BLOCK:(k+1)*BLOCK].T if k<first else g[c0:c0+BLOCK,k*BLOCK:(first+count)*BLOCK]]
        if rhs is not None: out.append(rhs[1][:,k*BLOCK:(k+1)*BLOCK].T)
        return jnp.concatenate(out,1) if len(out)>1 else out[0]
    for k in range(first):
        t=product(k,0)
        if k: t=t-mm(parts.column(k,k),w[:k*BLOCK,:all_cols],((0,),(0,)))
        u[k*BLOCK:(k+1)*BLOCK,:all_cols]=t
        w[k*BLOCK:(k+1)*BLOCK,:all_cols]=mm(parts.inverse(k),t)
    parts.add(first,count,u,w,inv)
    def early(k,done):
        c=(k-first)*BLOCK
        t=product(k,c)
        if done: t=t-mm(u[:done*BLOCK,c:c+BLOCK],w[:done*BLOCK,c:all_cols],((0,),(0,)))
        a[c:c+BLOCK,c:all_cols]=t
    early(first,first)
    for k in range(first,first+count):
        c=(k-first)*BLOCK
        if k+1<first+count: early(k+1,k)
        tiles=[]
        for v in range(BLOCK//8):
            t=a[c+8*v:c+8*v+8,c:c+BLOCK]
            tiles.append(jnp.where(lane-8*v==sub,t+ridge(k),t))
        block=jnp.concatenate(invert_block(tiles,q,s),0)
        inv[c:c+BLOCK,:]=block
        if c+BLOCK<all_cols:
            t=a[c:c+BLOCK,c+BLOCK:all_cols]
            r=mm(block,t)
            u[k*BLOCK:(k+1)*BLOCK,c+BLOCK:all_cols]=t
            w[k*BLOCK:(k+1)*BLOCK,c+BLOCK:all_cols]=r
            if k+1<first+count: a[c+BLOCK:c+2*BLOCK,c+BLOCK:all_cols]-=mm(t[:,:BLOCK],r,((0,),(0,)))

OFFSETS=(0,3,1,2)
def ridge_of(place_ref,ridge_ref):
    def ridge(k):
        at=(place_ref[0]+OFFSETS[k//2])%4*(2*BLOCK)+(k%2)*BLOCK
        return ridge_ref[0:1,pl.ds(pl.multiple_of(at,BLOCK),BLOCK)]
    return ridge

def halves(ref): return [ref.at[:ref.shape[0]//2,:],ref.at[ref.shape[0]//2:,:]]
def pieces(own,own_e,near=None,far=None):
    def of(k):
        if k<2: return [own[...],own_e[...]]
        if k<6: return [near[k//2-1][...],near[k//2+1][...]]
        n=far[0].shape[0]//2
        return [far[0][:n],far[1][:n],far[0][n:],far[1][n:]]
    return of

def first_kernel(q,s,place,own,own_e,ridge,u,w,inv,a,g):
    grow(Parts(),0,2,pieces(own,own_e),ridge_of(place,ridge),u,w,inv,a,g,q,s)

def second_kernel(q,s,place,own,own_e,below,above,near_e,ridge,u1,w1,i1,u,w,inv,a,g):
    parts=Parts(); parts.add(0,2,u1,w1,i1)
    n=own.shape[0]
    near=[below,above,near_e.at[:n,:],near_e.at[n:,:]]
    grow(parts,2,4,pieces(own,own_e,near),ridge_of(place,ridge),u,w,inv,a,g,q,s)

def third_kernel(q,s,place,own,own_e,below,above,near_e,far_a,far_b,ridge,u1,w1,i1,u2,w2,i2,d,o,u,w,inv,a,g,y,ct):
    parts=Parts(); parts.add(0,2,u1,w1,i1); parts.add(2,4,u2,w2,i2)
    n=own.shape[0]; x,core=place[0],place[1]
    near=[below,above,near_e.at[:n,:],near_e.at[n:,:]]
    of=pieces(own,own_e,near,(far_a,far_b))
    h=[jnp.concatenate(of(2*b),0) for b in range(4)]
    for side in range(2):
        for z0 in range(2):
            slot=2*z0+(core if side==0 else 1-core)
            starts=[side*n+(p*2+z0)*BLOCK for p in range(4)]
            rows=jnp.concatenate([jnp.concatenate([h[b][r:r+BLOCK,:] for b in range(4)],1) for r in starts],0)
            cols=jnp.concatenate([d[slot*4+(x+OFFSETS[b])%4] for b in range(4)],1)
            t=mm(cols,rows,((1,),(1,)),precision=None).astype(bf16)
            for p,r in enumerate(starts): y[:,r:r+BLOCK]=t[:,p*BLOCK:(p+1)*BLOCK]
    grow(parts,6,2,of,ridge_of(place,ridge),u,w,inv,a,g,q,s,rhs=(y,ct))
    nc=y.shape[0]; xs={}
    for k in range(7,-1,-1):
        t=w[k*BLOCK:(k+1)*BLOCK,2*BLOCK:2*BLOCK+nc]
        for first,count,_,ws,_ in reversed(parts.groups):
            lo=max(first,k+2); hi=first+count
            if lo<hi: t=t-mm(ws[k*BLOCK:(k+1)*BLOCK,(lo-first)*BLOCK:(hi-first)*BLOCK],jnp.concatenate([xs[j] for j in range(lo,hi)],0))
        if k<7:
            first,_,_,ws,_=parts.find(k+1); c=(k+1-first)*BLOCK
            t=t-mm(ws[k*BLOCK:(k+1)*BLOCK,c:c+BLOCK],xs[k+1])
        xs[k]=t
        at=(x+OFFSETS[k//2])%4*(2*BLOCK)+(k%2)*BLOCK
        o[:,pl.ds(pl.multiple_of(at,BLOCK),BLOCK)]=t.T

def call(kernel,outs,scratch,mib,gflop,args):
    vmem=pl.BlockSpec(memory_space=pltpu.VMEM)
    return pl.pallas_call(functools.partial(kernel,2,4),
        out_shape=[jax.ShapeDtypeStruct(o,f32) for o in outs],
        in_specs=[pl.BlockSpec(memory_space=pltpu.SMEM)]+[vmem]*(len(args)-1),out_specs=[vmem]*len(outs),
        scratch_shapes=scratch,cost_estimate=pl.CostEstimate(flops=int(gflop*1e9),bytes_accessed=1<<20,transcendentals=0),
        compiler_params=pltpu.CompilerParams(vmem_limit_bytes=mib*2**20))(*args)

def factor_own(place,own,own_e,ridge):
    return call(first_kernel,[(2*BLOCK,2*BLOCK)]*2+[(2*BLOCK,BLOCK)],[pltpu.VMEM((2*BLOCK,2*BLOCK),f32)]*2,20,8,(place,own,own_e,ridge))

def factor_near(place,own,own_e,below,above,near_e,ridge,state):
    return call(second_kernel,[(6*BLOCK,4*BLOCK)]*2+[(4*BLOCK,BLOCK)],[pltpu.VMEM((4*BLOCK,4*BLOCK),f32),pltpu.VMEM((4*BLOCK,6*BLOCK),f32)],20,16,(place,own,own_e,below,above,near_e,ridge,*state))

def finish(place,own,own_e,below,above,near_e,far_a,far_b,ridge,state1,state2,d):
    n=2*own.shape[0]; nc=d.shape[1]
    wide=pltpu.VMEM((8*BLOCK,3*BLOCK),f32)
    return call(third_kernel,[(nc,8*BLOCK)],[wide,wide,pltpu.VMEM((2*BLOCK,BLOCK),f32),wide,pltpu.VMEM((2*BLOCK,8*BLOCK),f32),pltpu.VMEM((nc,n),bf16),pltpu.VMEM((nc,8*BLOCK),f32)],20,12,
        (place,own,own_e,below,above,near_e,far_a,far_b,ridge,*state1,*state2,d))[0]


def shifted(a, axis, distance):
    n = lax.axis_size(axis)
    return lax.ppermute(a, axis, [(i, (i + distance) % n) for i in range(n)])


def per_device(tokens, routes, member_expert, gate_weight, up_weight, down_weight, ridge):
    count, width = tokens.shape
    hidden = gate_weight.shape[1]
    cap, quarter = 4, width // 4
    down = down_weight.reshape(hidden, 16, 64).transpose(1, 2, 0)
    down = lax.all_to_all(down, ("z0", "core", "x"), 0, 0, tiled=True)
    chosen = jnp.any(routes[:, :, None] == member_expert[None, None, :], axis=1).astype(f32)
    triangle = jnp.tril(jnp.ones((count, count), f32))
    position = jnp.dot(triangle, chosen, preferred_element_type=f32) - 1.0
    selector = chosen.T[:, None, :] * (
        position.T[:, None, :] == jnp.arange(cap, dtype=f32)[None, :, None]
    )
    outgoing = jnp.einsum(
        "cist,tqd->cqisd",
        selector.astype(bf16).reshape(8, 4, cap, count),
        tokens.reshape(count, 4, quarter),
        preferred_element_type=f32,
    )
    outgoing = outgoing.astype(bf16).reshape(128, cap, quarter)
    received = lax.all_to_all(outgoing, EXPERT, 0, 0, tiled=True)
    slot_rows = received.reshape(128 * cap, quarter)
    gate = jnp.dot(slot_rows, gate_weight, preferred_element_type=f32)
    up = jnp.dot(slot_rows, up_weight, preferred_element_type=f32)
    partial = jnp.concatenate([gate, up], 1)
    span = partial.shape[0] // 4
    parts = lax.all_to_all(partial, "p", 0, 0, tiled=True)
    total = jnp.sum(parts.reshape(4, span, 2 * hidden), axis=0)
    h_own = (jax.nn.silu(total[:, :hidden]) * total[:, hidden:]).astype(bf16)
    copies = jnp.broadcast_to(h_own[None], (8, span, hidden)).reshape(8 * span, hidden)
    own = lax.all_to_all(copies, ("p", "z0"), 0, 0, tiled=True)
    from_below, from_above = shifted(own, "x", 1), shifted(own, "x", -1)
    own_e = shifted(own, "core", 1)
    place = jnp.stack([lax.axis_index("x"), lax.axis_index("core")]).astype(jnp.int32)
    ridge = ridge.reshape(1, 4 * hidden)
    state1 = factor_own(place, own, own_e, ridge)
    from_below, from_above, state1 = lax.optimization_barrier((from_below, from_above, state1))
    near_e = shifted(jnp.concatenate([from_below, from_above], 0), "core", 1)
    half = 4 * span
    far_a = shifted(jnp.concatenate([from_below[:half], near_e[:half]], 0), "x", 1)
    far_b = shifted(jnp.concatenate([from_above[half:], near_e[3 * half :]], 0), "x", -1)
    near = (place, own, own_e, from_below, from_above, near_e)
    state2 = factor_near(*near, ridge, state1)
    return finish(*near, far_a, far_b, ridge, state1, state2, down)


def solution(mesh):
    fine = Mesh(mesh.devices.reshape(8, 4, 2, 2, 4), ("y", "p", "z0", "core", "x"))
    in_specs = (
        P(EXPERT, None),
        P(EXPERT, None),
        P(),
        P(EXPERT, "x"),
        P(EXPERT, "x"),
        P("x", EXPERT),
        P(),
    )
    return jax.shard_map(
        per_device,
        mesh=fine,
        in_specs=in_specs,
        out_specs=P(EXPERT + ("x",), None),
        check_vma=False,
    )
```

```python
import functools

import jax
import jax.numpy as jnp
from jax import lax
from jax.experimental import pallas as pl
from jax.experimental.pallas import tpu as pltpu
from jax.sharding import Mesh
from jax.sharding import PartitionSpec as P

f32 = jnp.float32
bf16 = jnp.bfloat16
EXPERT = ("y", "p", "z0", "core")
BLOCK = 128


def sub_bc(v,k): return jnp.broadcast_to(v[k:k+1,:],v.shape)
def lane_bc(v,m): return jnp.broadcast_to(v[:,m:m+1],v.shape)
def tree_sum(t):
    while len(t)>1: t=[t[i]+t[i+1] for i in range(0,len(t)-1,2)]+([t[-1]] if len(t)%2 else [])
    return t[0]
def mm(a,b,dims=((1,),(0,)),precision=lax.Precision.HIGHEST):
    return lax.dot_general(a,b,(dims,((),())),preferred_element_type=f32,precision=precision)

def panel_step(rows,own,others,j0,sub,lane):
    q=len(own); w=8*q
    cols=[[lane_bc(rows[v],j0+m) for v in own] for m in range(w)]
    mult={v:[lane_bc(rows[v],j0+m) for m in range(w)] for v in others}
    panel=(lane>=j0)&(lane<j0+w)
    top=[jnp.where(panel,(lane-j0-8*a==sub).astype(f32),rows[v]) for a,v in enumerate(own)]
    for k in range(w):
        ka,ks=divmod(k,8)
        here=sub==ks
        r=1.0/sub_bc(cols[k][ka],ks)
        piv=[(jnp.where(here,-1.0,c) if a==ka else c) for a,c in enumerate(cols[k])]
        pr=[c*r for c in piv]
        def step(vs,late=False):
            t=sub_bc(vs[ka],ks)
            x0=[jnp.where(here,0.0,x) if a==ka else x for a,x in enumerate(vs)]
            if late: return [x-(piv[a]*t)*r for a,x in enumerate(x0)]
            return [x-pr[a]*t for a,x in enumerate(x0)]
        for m in range(k+1,w): cols[m]=step(cols[m],m==k+1)
        top=step(top)
    for a,v in enumerate(own): rows[v]=top[a]
    if others:
        spread=[sub_bc(top[m//8],m%8) for m in range(w)]
        for v in others:
            rows[v]=jnp.where(panel,0.0,rows[v])-tree_sum([mult[v][m]*spread[m] for m in range(w)])

def invert_block(rows,q,s):
    n=len(rows); rows=list(rows)
    sub=lax.broadcasted_iota(jnp.int32,(8,BLOCK),0); lane=lax.broadcasted_iota(jnp.int32,(8,BLOCK),1)
    for a in range(0,n,s):
        strip=list(range(a,a+s)); ahead=list(range(a+s,min(a+s+q,n)))
        mult={v:[lane_bc(rows[v],8*a+m) for m in range(8*s)] for v in ahead}
        for t in range(a,a+s,q):
            own=list(range(t,t+q))
            panel_step(rows,own,[v for v in strip if v not in own],8*t,sub,lane)
        inst=(lane>=8*a)&(lane<8*(a+s))
        z=jnp.zeros((8,BLOCK),f32)
        wide=jnp.concatenate([rows[v] if v in strip else z for v in range(n)],0)
        spread=[sub_bc(rows[a+m//8],m%8) for m in range(8*s)]
        rest=[v for v in range(n) if v not in strip and v not in ahead]
        for v in ahead:
            rows[v]=jnp.where(inst,0.0,rows[v])-tree_sum([mult[v][m]*spread[m] for m in range(8*s)])
        if rest:
            upd=mm(jnp.concatenate([rows[v] for v in rest],0),wide)
            for i,v in enumerate(rest): rows[v]=jnp.where(inst,0.0,rows[v])-upd[8*i:8*i+8]
    return rows

    return rows


class Parts:
    def __init__(self): self.groups=[]
    def add(self,first,count,w,inv): self.groups.append((first,count,w,inv))
    def find(self,k): return next(g for g in self.groups if g[0]<=k<g[0]+g[1])
    def column(self,k,rows):
        g=self.find(k); c=(k-g[0])*BLOCK
        return g[2][:rows*BLOCK,c:c+BLOCK]
    def inverse(self,k):
        g=self.find(k); r=(k-g[0])*BLOCK
        return g[3][r:r+BLOCK,:]

def gather(pieces,c0,c1): return jnp.concatenate([p[:,c0:c1] for p in pieces],0)

def grow(parts,first,count,pieces_of,ridge,u,w,inv,a,g,q,s,rhs=None):
    sub=lax.broadcasted_iota(jnp.int32,(8,BLOCK),0); lane=lax.broadcasted_iota(jnp.int32,(8,BLOCK),1)
    wide=count*BLOCK; all_cols=wide+(rhs[0].shape[0] if rhs is not None else 0)
    turned=jnp.concatenate([gather(pieces_of(first+2*j),0,2*BLOCK) for j in range(count//2)],1).T
    for b in range((first+count)//2):
        g[:,2*b*BLOCK:2*(b+1)*BLOCK]=mm(turned,gather(pieces_of(2*b),0,2*BLOCK),precision=None)
        if rhs is not None: rhs[1][:,2*b*BLOCK:2*(b+1)*BLOCK]=mm(rhs[0][...],gather(pieces_of(2*b),0,2*BLOCK),precision=None)
    def product(k,c0):
        out=[g[:,k*BLOCK:(k+1)*BLOCK].T if k<first else g[c0:c0+BLOCK,k*BLOCK:(first+count)*BLOCK]]
        if rhs is not None: out.append(rhs[1][:,k*BLOCK:(k+1)*BLOCK].T)
        return jnp.concatenate(out,1) if len(out)>1 else out[0]
    for k in range(first):
        t=product(k,0)
        if k: t=t-mm(parts.column(k,k),u[:k*BLOCK,:all_cols],((0,),(0,)))
        u[k*BLOCK:(k+1)*BLOCK,:all_cols]=t
        w[k*BLOCK:(k+1)*BLOCK,:all_cols]=mm(parts.inverse(k),t)
    parts.add(first,count,w,inv)
    def early(k,done):
        c=(k-first)*BLOCK
        t=product(k,c)
        if done: t=t-mm(u[:done*BLOCK,c:c+BLOCK],w[:done*BLOCK,c:all_cols],((0,),(0,)))
        a[c:c+BLOCK,c:all_cols]=t
    early(first,first)
    for k in range(first,first+count):
        c=(k-first)*BLOCK
        if k+1<first+count: early(k+1,k)
        tiles=[]
        for v in range(BLOCK//8):
            t=a[c+8*v:c+8*v+8,c:c+BLOCK]
            tiles.append(jnp.where(lane-8*v==sub,t+ridge(k),t))
        block=jnp.concatenate(invert_block(tiles,q,s),0)
        inv[c:c+BLOCK,:]=block
        if c+BLOCK<all_cols:
            last=k+1==first+count
            near=min(c+2*BLOCK,all_cols)
            t=a[c:c+BLOCK,c+BLOCK:near]
            r=mm(block,t)
            u[k*BLOCK:(k+1)*BLOCK,c+BLOCK:near]=t
            w[k*BLOCK:(k+1)*BLOCK,c+BLOCK:near]=r
            if not last: a[c+BLOCK:c+2*BLOCK,c+BLOCK:near]-=mm(t,r,((0,),(0,)))
            if near<all_cols:
                more=a[c:c+BLOCK,near:all_cols]
                r=mm(block,more)
                u[k*BLOCK:(k+1)*BLOCK,near:all_cols]=more
                w[k*BLOCK:(k+1)*BLOCK,near:all_cols]=r
                if not last: a[c+BLOCK:c+2*BLOCK,near:all_cols]-=mm(t,r,((0,),(0,)))

OFFSETS=(0,3,1,2)
def ridge_of(place_ref,ridge_ref):
    def ridge(k):
        at=(place_ref[0]+OFFSETS[k//2])%4*(2*BLOCK)+(k%2)*BLOCK
        return ridge_ref[0:1,pl.ds(pl.multiple_of(at,BLOCK),BLOCK)]
    return ridge

def halves(ref): return [ref.at[:ref.shape[0]//2,:],ref.at[ref.shape[0]//2:,:]]
def pieces(own,own_e,near=None,far=None):
    def of(k):
        if k<2: return [own[...],own_e[...]]
        if k<6: return [near[k//2-1][...],near[k//2+1][...]]
        n=far[0].shape[0]//2
        return [far[0][:n],far[1][:n],far[0][n:],far[1][n:]]
    return of

def first_kernel(q,s,place,own,own_e,ridge,w,inv,u,a,g):
    grow(Parts(),0,2,pieces(own,own_e),ridge_of(place,ridge),u,w,inv,a,g,q,s)

def second_kernel(q,s,place,own,own_e,below,above,near_e,ridge,w1,i1,w,inv,u,a,g):
    parts=Parts(); parts.add(0,2,w1,i1)
    n=own.shape[0]
    near=[below,above,near_e.at[:n,:],near_e.at[n:,:]]
    grow(parts,2,4,pieces(own,own_e,near),ridge_of(place,ridge),u,w,inv,a,g,q,s)

def third_kernel(q,s,place,own,own_e,below,above,near_e,far_a,far_b,ridge,w1,i1,w2,i2,d,o,u,w,inv,a,g,y,ct):
    parts=Parts(); parts.add(0,2,w1,i1); parts.add(2,4,w2,i2)
    n=own.shape[0]; x,core=place[0],place[1]
    near=[below,above,near_e.at[:n,:],near_e.at[n:,:]]
    of=pieces(own,own_e,near,(far_a,far_b))
    h=[jnp.concatenate(of(2*b),0) for b in range(4)]
    for side in range(2):
        for z0 in range(2):
            slot=2*z0+(core if side==0 else 1-core)
            starts=[side*n+(p*2+z0)*BLOCK for p in range(4)]
            rows=jnp.concatenate([jnp.concatenate([h[b][r:r+BLOCK,:] for b in range(4)],1) for r in starts],0)
            cols=jnp.concatenate([d[slot*4+(x+OFFSETS[b])%4] for b in range(4)],1)
            t=mm(cols,rows,((1,),(1,)),precision=None).astype(bf16)
            for p,r in enumerate(starts): y[:,r:r+BLOCK]=t[:,p*BLOCK:(p+1)*BLOCK]
    grow(parts,6,2,of,ridge_of(place,ridge),u,w,inv,a,g,q,s,rhs=(y,ct))
    nc=y.shape[0]; xs={}
    for k in range(7,-1,-1):
        t=w[k*BLOCK:(k+1)*BLOCK,2*BLOCK:2*BLOCK+nc]
        for first,count,ws,_ in reversed(parts.groups):
            lo=max(first,k+2); hi=first+count
            if lo<hi: t=t-mm(ws[k*BLOCK:(k+1)*BLOCK,(lo-first)*BLOCK:(hi-first)*BLOCK],jnp.concatenate([xs[j] for j in range(lo,hi)],0))
        if k<7:
            first,_,ws,_=parts.find(k+1); c=(k+1-first)*BLOCK
            t=t-mm(ws[k*BLOCK:(k+1)*BLOCK,c:c+BLOCK],xs[k+1])
        xs[k]=t
        at=(x+OFFSETS[k//2])%4*(2*BLOCK)+(k%2)*BLOCK
        o[:,pl.ds(pl.multiple_of(at,BLOCK),BLOCK)]=t.T

def call(kernel,outs,scratch,gflop,args):
    vmem=pl.BlockSpec(memory_space=pltpu.VMEM)
    return pl.pallas_call(functools.partial(kernel,2,4),
        out_shape=[jax.ShapeDtypeStruct(o,f32) for o in outs],
        in_specs=[pl.BlockSpec(memory_space=pltpu.SMEM)]+[vmem]*(len(args)-1),out_specs=[vmem]*len(outs),
        scratch_shapes=scratch,cost_estimate=pl.CostEstimate(flops=int(gflop*1e9),bytes_accessed=1<<20,transcendentals=0),
        compiler_params=pltpu.CompilerParams(vmem_limit_bytes=24*2**20))(*args)

def factor_own(place,own,own_e,ridge):
    return call(first_kernel,[(2*BLOCK,2*BLOCK),(2*BLOCK,BLOCK)],[pltpu.VMEM((2*BLOCK,2*BLOCK),f32)]*3,8,(place,own,own_e,ridge))

def factor_near(place,own,own_e,below,above,near_e,ridge,state):
    return call(second_kernel,[(6*BLOCK,4*BLOCK),(4*BLOCK,BLOCK)],
        [pltpu.VMEM((6*BLOCK,4*BLOCK),f32),pltpu.VMEM((4*BLOCK,4*BLOCK),f32),pltpu.VMEM((4*BLOCK,6*BLOCK),f32)],16,
        (place,own,own_e,below,above,near_e,ridge,*state))

def finish(place,own,own_e,below,above,near_e,far_a,far_b,ridge,state1,state2,d):
    n=2*own.shape[0]; nc=d.shape[1]
    wide=pltpu.VMEM((8*BLOCK,3*BLOCK),f32)
    return call(third_kernel,[(nc,8*BLOCK)],
        [wide,wide,pltpu.VMEM((2*BLOCK,BLOCK),f32),wide,pltpu.VMEM((2*BLOCK,8*BLOCK),f32),pltpu.VMEM((nc,n),bf16),pltpu.VMEM((nc,8*BLOCK),f32)],12,
        (place,own,own_e,below,above,near_e,far_a,far_b,ridge,*state1,*state2,d))[0]


def shifted(a, axis, distance):
    n = lax.axis_size(axis)
    return lax.ppermute(a, axis, [(i, (i + distance) % n) for i in range(n)])


def per_device(tokens, routes, member_expert, gate_weight, up_weight, down_weight, ridge):
    count, width = tokens.shape
    hidden = gate_weight.shape[1]
    cap, quarter = 4, width // 4
    down = down_weight.reshape(hidden, 16, 64).transpose(1, 2, 0)
    down = lax.all_to_all(down, ("z0", "core", "x"), 0, 0, tiled=True)
    chosen = jnp.any(routes[:, :, None] == member_expert[None, None, :], axis=1).astype(f32)
    triangle = jnp.tril(jnp.ones((count, count), f32))
    position = jnp.dot(triangle, chosen, preferred_element_type=f32) - 1.0
    selector = chosen.T[:, None, :] * (
        position.T[:, None, :] == jnp.arange(cap, dtype=f32)[None, :, None]
    )
    outgoing = jnp.einsum(
        "cist,tqd->cqisd",
        selector.astype(bf16).reshape(8, 4, cap, count),
        tokens.reshape(count, 4, quarter),
        preferred_element_type=f32,
    )
    outgoing = outgoing.astype(bf16).reshape(128, cap, quarter)
    received = lax.all_to_all(outgoing, EXPERT, 0, 0, tiled=True)
    slot_rows = received.reshape(128 * cap, quarter)
    gate = jnp.dot(slot_rows, gate_weight, preferred_element_type=f32)
    up = jnp.dot(slot_rows, up_weight, preferred_element_type=f32)
    partial = jnp.concatenate([gate, up], 1)
    span = partial.shape[0] // 4
    parts = lax.all_to_all(partial, "p", 0, 0, tiled=True)
    total = jnp.sum(parts.reshape(4, span, 2 * hidden), axis=0)
    h_own = (jax.nn.silu(total[:, :hidden]) * total[:, hidden:]).astype(bf16)
    copies = jnp.broadcast_to(h_own[None], (8, span, hidden)).reshape(8 * span, hidden)
    own = lax.all_to_all(copies, ("p", "z0"), 0, 0, tiled=True)
    from_below, from_above = shifted(own, "x", 1), shifted(own, "x", -1)
    own_e = shifted(own, "core", 1)
    place = jnp.stack([lax.axis_index("x"), lax.axis_index("core")]).astype(jnp.int32)
    ridge = ridge.reshape(1, 4 * hidden)
    state1 = factor_own(place, own, own_e, ridge)
    from_below, from_above, state1 = lax.optimization_barrier((from_below, from_above, state1))
    near_e = shifted(jnp.concatenate([from_below, from_above], 0), "core", 1)
    half = 4 * span
    far_a = shifted(jnp.concatenate([from_below[:half], near_e[:half]], 0), "x", 1)
    far_b = shifted(jnp.concatenate([from_above[half:], near_e[3 * half :]], 0), "x", -1)
    near = (place, own, own_e, from_below, from_above, near_e)
    state2 = factor_near(*near, ridge, state1)
    return finish(*near, far_a, far_b, ridge, state1, state2, down)


def solution(mesh):
    fine = Mesh(mesh.devices.reshape(8, 4, 2, 2, 4), ("y", "p", "z0", "core", "x"))
    in_specs = (
        P(EXPERT, None),
        P(EXPERT, None),
        P(),
        P(EXPERT, "x"),
        P(EXPERT, "x"),
        P("x", EXPERT),
        P(),
    )
    return jax.shard_map(
        per_device,
        mesh=fine,
        in_specs=in_specs,
        out_specs=P(EXPERT + ("x",), None),
        check_vma=False,
    )
```
